256 devices in a mesh: section: 4 (over z_lo, core), dp: 64 (over z_hi, y, x).
Axes of the slice: x: 4, y: 4, z: 8 (z_hi: 4, z_lo: 2; z = z_hi * 2 + z_lo), core: 2. Of those that a mesh axis runs over, the one named last changes fastest.
Arguments:
- activations: bfloat16 [4, 4, 3584, 6144], P('section', None, 'dp'), may hold values from -16 to 16
- top_cotangent: bfloat16 [4, 3584, 6144], P(None, 'dp'), may hold values from -16 to 16
- branch_gains: float32 [4, 6144], P('section'), may hold values from 0.5 to 1.5
Outputs:
- input_factor: float32 [4, 6144, 384], P('section', 'dp')
- grad_factor: float32 [4, 6144, 384], P('section', 'dp')
The draws below stay inside these ranges and needn't reach their ends.
All inputs are finite; a program needn't handle non-finite values.
Results may differ from the reference program's by a relative error of at most 0.0037.
Values may be sent and summed in bfloat16 or wider, within the bound.
A program may use at most 128 MiB of HBM per device.

```python
import jax
import jax.numpy as jnp
from jax import lax

D = 6144
MICRO = 4
PANEL = 384
TOKENS = 3584
N_SECTION = 4


def with_spikes(values, stream_key, source, target, shards_of, factor):
    def block_of(position):
        return (jnp.arange(values.shape[position]) // (values.shape[position] // shards_of)).reshape((-1,) + (1,) * (values.ndim - 1 - position))

    near = jax.random.permutation(stream_key, shards_of)[block_of(target)]
    other_side = (block_of(target) + shards_of // 2) % shards_of
    return jnp.where((block_of(source) == near) | (block_of(source) == other_side), factor * values, values)


def shard_levels(key, extent, shards, low, largest):
    factor_of = 1.0
    for axis_at, parts in shards:
        steps = jax.random.uniform(jax.random.fold_in(jax.random.fold_in(key, 6), axis_at), (parts,), jnp.float32, low / len(shards), largest / len(shards))
        factor_of = factor_of * jnp.repeat(jnp.exp(steps), extent[axis_at] // parts).reshape((-1,) + (1,) * (len(extent) - 1 - axis_at))
    return factor_of


def bell_draw_with(stream_key, dims, width, limit, cuts, heavy, kind=jnp.bfloat16):
    array = width * jax.random.normal(stream_key, dims, jnp.float32)
    if cuts:
        array = array * shard_levels(stream_key, dims, cuts, -0.22, 0.18)
    return jnp.clip(with_spikes(array, jax.random.fold_in(stream_key, 3), *heavy), -limit, limit).astype(kind)


def setup_inputs(seed: int = 0) -> dict:
    splits = jax.random.split(jax.random.key(seed), 4)
    activations = bell_draw_with(splits[0], (N_SECTION, MICRO, TOKENS, D), 1.0, 16.0, ((0, 4), (2, 64)), (2, 3, 64, 4.0))
    top_cotangent = bell_draw_with(splits[1], (MICRO, TOKENS, D), 1.0, 16.0, ((1, 64),), (1, 2, 64, 4.0))
    branch_gains = jnp.clip(0.5 + 1.0 * jax.random.uniform(splits[2], (N_SECTION, D), jnp.float32) ** shard_levels(splits[2], (N_SECTION, D), ((0, 4),), -0.2, 0.2), 0.5, 1.5)
    return dict(activations=activations, top_cotangent=top_cotangent, branch_gains=branch_gains)


def gelu_slope(values):
    return 0.5 * (1.0 + lax.erf(values * 0.7071067811865476)) + values * jnp.exp(-0.5 * values * values) * 0.3989422804014327


def reference(activations, top_cotangent, branch_gains):
    row_count = MICRO * TOKENS
    cotangent = top_cotangent.reshape(row_count, D)
    input_parts = []
    grad_parts = []
    for layer_index in range(N_SECTION - 1, -1, -1):
        flat_input = activations[layer_index].reshape(row_count, D)
        input_parts.append(jnp.dot(flat_input.T, flat_input[:, :PANEL], preferred_element_type=jnp.float32) / jnp.float32(row_count))
        grad_parts.append(jnp.dot(cotangent.T, cotangent[:, :PANEL], preferred_element_type=jnp.float32) / jnp.float32(row_count))
        slope = gelu_slope(flat_input.astype(jnp.float32))
        scaling = 1.0 + branch_gains[layer_index][None, :] * slope
        cotangent = (cotangent.astype(jnp.float32) * scaling).astype(jnp.bfloat16)
    input_factor = jnp.stack(input_parts[::-1], axis=0)
    grad_factor = jnp.stack(grad_parts[::-1], axis=0)
    return (input_factor, grad_factor)
```

```python
import jax
import jax.numpy as jnp
from jax import lax
from jax.experimental import pallas as pl
from jax.experimental.pallas import tpu as pltpu
from jax.sharding import PartitionSpec as P

PANEL = 384
ROWS = 224
BLOCKS = 16
SLAB = 32
MESH = pl.DeviceIdType.MESH
F32 = jnp.float32
BF16 = jnp.bfloat16


def gelu_slope(values):
    return (
        0.5 * (1.0 + lax.erf(values * 0.7071067811865476))
        + values * jnp.exp(-0.5 * values * values) * 0.3989422804014327
    )


def kernel(
    total_rows,
    x_hbm,
    top_hbm,
    gains,
    in_out,
    grad_out,
    xbuf,
    cbuf,
    obuf,
    held,
    part,
    bsend,
    brecv,
    csend,
    crecv,
    fin,
    x_load,
    c_in,
    relay_sent,
    a_sent,
    a_in,
    b_sent,
    b_in,
    c_sent,
    c_got,
):
    s = lax.axis_index("section")
    d = lax.axis_index("dp")
    core = s % 2
    zh, y, x = d // 16, (d // 4) % 4, d % 4
    a = jnp.where(core == 0, y, x)
    b = jnp.where(core == 0, x, y)

    def at(zz, aa, bb):
        return zz * 16 + jnp.where(core == 0, aa * 4 + bb, bb * 4 + aa)

    def peer_a(aa):
        return (s, at(zh, aa, b))

    def peer_b(bb):
        return (s, at(zh, a, bb))

    def owner(zz):
        return (s, zz * 16 + a * 4 + b)

    swapped = jnp.logical_and(core == 1, a != b)
    straight = jnp.logical_not(swapped)

    barrier = pltpu.get_barrier_semaphore()

    def greet(device):
        pl.semaphore_signal(barrier, inc=1, device_id=device, device_id_type=MESH)

    for o in (1, 2, 3):
        greet(peer_a((a + o) % 4))
        greet(peer_b((b + o) % 4))
        greet(owner((zh + o) % 4))

    @pl.when(swapped)
    def _():
        greet(owner(zh))

    @pl.when(s > 0)
    def _():
        greet((s - 1, d))

    @pl.when(s < 3)
    def _():
        greet((s + 1, d))

    first = 4 * (3 - zh) + (8 - x - y) % 4

    def block_at(p):
        i = jnp.where(p == 0, first, jnp.where(p <= first, p - 1, p))
        return ((zh + 1 + i // 4) % 4) * 4 + (i + x + y) % 4

    def columns(blk):
        return pl.ds(pl.multiple_of(blk * PANEL, PANEL), PANEL)

    def rows_of(aa):
        return pl.ds(pl.multiple_of(aa * ROWS, ROWS), ROWS)

    def load(p, _):
        blk = block_at(p)

        @pl.when(s > 0)
        def _():
            pltpu.make_async_copy(x_hbm.at[:, columns(blk)], xbuf.at[blk], x_load.at[blk]).start()

        @pl.when(s == 3)
        def _():
            pltpu.make_async_copy(top_hbm.at[:, columns(blk)], cbuf.at[blk], c_in.at[blk]).start()

        return 0

    lax.fori_loop(0, BLOCKS, load, 0)

    others = 9 + jnp.where(swapped, 1, 0) + jnp.where(s > 0, 1, 0) + jnp.where(s < 3, 1, 0)
    pl.semaphore_wait(barrier, others)

    def to_peer(f, src, slot, sent, aa):
        return pltpu.make_async_remote_copy(
            src_ref=src,
            dst_ref=held.at[f, slot, rows_of(a), :],
            send_sem=a_sent.at[f, sent],
            recv_sem=a_in.at[f, slot, a],
            device_id=peer_a(aa),
            device_id_type=MESH,
        )

    def keep(f, src, slot):
        return pltpu.make_async_copy(src, held.at[f, slot, rows_of(a), :], a_in.at[f, slot, a])

    def sends_block(zz, aa):
        return jnp.logical_or(zz != 0, aa != 0)

    panel_src = x_hbm.at[:, pl.ds(0, PANEL)]
    for o in (2, 1, 3):
        to_peer(0, panel_src, 4, 16 + o, (a + o) % 4).start()
    keep(0, panel_src, 4).start()

    def send_x(j, _):
        zz = (zh + 1 + j) % 4
        for o in (2, 1, 3):
            aa = (a + o) % 4
            blk = zz * 4 + aa

            @pl.when(sends_block(zz, aa))
            def _():
                to_peer(0, x_hbm.at[:, columns(blk)], zz, blk, aa).start()

        @pl.when(sends_block(zz, a))
        def _():
            keep(0, x_hbm.at[:, columns(zz * 4 + a)], zz).start()

        return 0

    lax.fori_loop(0, 4, send_x, 0)

    def relay_copy(blk):
        return pltpu.make_async_remote_copy(
            src_ref=obuf.at[blk],
            dst_ref=cbuf.at[blk],
            send_sem=relay_sent.at[blk],
            recv_sem=c_in.at[blk],
            device_id=(s - 1, d),
            device_id_type=MESH,
        )

    def relay(p, _):
        blk = block_at(p)
        zz, q = blk // 4, blk % 4
        pltpu.make_async_copy(cbuf.at[blk], cbuf.at[blk], c_in.at[blk]).wait()

        @pl.when(p == 0)
        def _():
            for o in (2, 1, 3):
                to_peer(1, cbuf.at[blk], 4, 16 + o, (a + o) % 4).start()
            keep(1, cbuf.at[blk], 4).start()

        @pl.when(jnp.logical_and(p > 0, q != a))
        def _():
            to_peer(1, cbuf.at[blk], zz, blk, q).start()

        @pl.when(jnp.logical_and(p > 0, q == a))
        def _():
            keep(1, cbuf.at[blk], zz).start()

        @pl.when(s > 0)
        def _():
            pltpu.make_async_copy(xbuf.at[blk], xbuf.at[blk], x_load.at[blk]).wait()
            gain = gains[blk]

            def slab(i, _):
                rows = pl.ds(pl.multiple_of(i * SLAB, SLAB), SLAB)
                scaling = 1.0 + gain * gelu_slope(xbuf[blk, rows, :].astype(F32))
                obuf[blk, rows, :] = (cbuf[blk, rows, :].astype(F32) * scaling).astype(BF16)
                return 0

            lax.fori_loop(0, ROWS // SLAB, slab, 0)
            relay_copy(blk).start()

        return 0

    def await_slot(f, slot):
        for aa in range(4):
            there = held.at[f, slot, pl.ds(aa * ROWS, ROWS), :]
            pltpu.make_async_copy(there, there, a_in.at[f, slot, aa]).wait()

    def b_copy(f, j, o):
        bb = (b + o) % 4
        return pltpu.make_async_remote_copy(
            src_ref=bsend.at[f, j, bb],
            dst_ref=brecv.at[f, j, o - 1],
            send_sem=b_sent.at[f, j, o - 1],
            recv_sem=b_in.at[f, j, o - 1],
            device_id=peer_b(bb),
            device_id_type=MESH,
        )

    def gram(f, j):
        zz = (zh + 1 + j) % 4
        slot = jnp.where(sends_block(zz, a), zz, 4)
        if j == 0:
            await_slot(f, 4)

        @pl.when(sends_block(zz, a))
        def _():
            await_slot(f, zz)

        part[f, j] = lax.dot_general(
            held[f, slot], held[f, 4], (((0,), (0,)), ((), ())), preferred_element_type=F32
        )
        for bb in range(4):
            bsend[f, j, bb] = part[f, j, pl.ds(bb * 96, 96), :].astype(BF16)
        for o in (2, 1, 3):
            b_copy(f, j, o).start()

    def c_copy(f, j):
        return pltpu.make_async_remote_copy(
            src_ref=csend.at[f, j],
            dst_ref=crecv.at[f, j],
            send_sem=c_sent.at[f, j],
            recv_sem=c_got.at[f, j],
            device_id=owner((zh + 1 + j) % 4),
            device_id_type=MESH,
        )

    def sum_b(f, j):
        total = part[f, j, pl.ds(pl.multiple_of(b * 96, 96), 96), :]
        for o in (1, 3, 2):
            b_copy(f, j, o).wait_recv()
            total = total + brecv[f, j, o - 1].astype(F32)
        if j < 3:
            csend[f, j] = total.astype(BF16)
            c_copy(f, j).start()
        else:
            fin[f] = total

            @pl.when(swapped)
            def _():
                csend[f, j] = total.astype(BF16)
                c_copy(f, j).start()

    def finish(f, out):
        @pl.when(swapped)
        def _():
            c_copy(f, 3).wait_recv()
            fin[f] = crecv[f, 3].astype(F32)

        total = fin[f]
        for j in range(3):
            c_copy(f, j).wait_recv()
            total = total + crecv[f, j].astype(F32)
        out[0] = total / F32(total_rows)

    def relays(low, high):
        lax.fori_loop(low, high, relay, 0)

    relays(0, 7)
    gram(0, 0)
    relays(7, 9)
    gram(0, 1)
    sum_b(0, 0)
    relays(9, 11)
    gram(0, 2)
    sum_b(0, 1)
    relays(11, 13)
    gram(0, 3)
    gram(1, 0)
    sum_b(0, 2)
    relays(13, 15)
    gram(1, 1)
    sum_b(0, 3)
    relays(15, 16)
    sum_b(1, 0)
    gram(1, 2)
    sum_b(1, 1)
    finish(0, in_out)
    gram(1, 3)
    sum_b(1, 2)
    sum_b(1, 3)
    finish(1, grad_out)

    for f in range(2):
        for o in (1, 2, 3):
            to_peer(f, cbuf.at[0], 4, 16 + o, (a + o) % 4).wait_send()

        def sent(blk, _):
            q = blk % 4

            @pl.when(jnp.logical_and(blk > 0, q != a))
            def _():
                to_peer(f, cbuf.at[blk], blk // 4, blk, q).wait_send()

            return 0

        lax.fori_loop(0, BLOCKS, sent, 0)
        for j in range(4):
            for o in (1, 2, 3):
                b_copy(f, j, o).wait_send()
        for j in range(3):
            c_copy(f, j).wait_send()

        @pl.when(swapped)
        def _():
            c_copy(f, 3).wait_send()

    @pl.when(s > 0)
    def _():
        def relayed(blk, _):
            relay_copy(blk).wait_send()
            return 0

        lax.fori_loop(0, BLOCKS, relayed, 0)


def body(activations, top_cotangent, branch_gains):
    width = activations.shape[-1]
    total_rows = ROWS * lax.axis_size("dp")
    dma = pltpu.SemaphoreType.DMA
    return pl.pallas_call(
        lambda *refs: kernel(total_rows, *refs),
        out_shape=[jax.ShapeDtypeStruct((1, 96, PANEL), F32)] * 2,
        in_specs=[
            pl.BlockSpec(memory_space=pl.ANY),
            pl.BlockSpec(memory_space=pl.ANY),
            pl.BlockSpec(memory_space=pltpu.VMEM),
        ],
        out_specs=[pl.BlockSpec(memory_space=pltpu.VMEM)] * 2,
        scratch_shapes=[
            pltpu.VMEM((BLOCKS, ROWS, PANEL), BF16),
            pltpu.VMEM((BLOCKS, ROWS, PANEL), BF16),
            pltpu.VMEM((BLOCKS, ROWS, PANEL), BF16),
            pltpu.VMEM((2, 5, 4 * ROWS, PANEL), BF16),
            pltpu.VMEM((2, 4, PANEL, PANEL), F32),
            pltpu.VMEM((2, 4, 4, 96, PANEL), BF16),
            pltpu.VMEM((2, 4, 3, 96, PANEL), BF16),
            pltpu.VMEM((2, 4, 96, PANEL), BF16),
            pltpu.VMEM((2, 4, 96, PANEL), BF16),
            pltpu.VMEM((2, 96, PANEL), F32),
            dma((BLOCKS,)),
            dma((BLOCKS,)),
            dma((BLOCKS,)),
            dma((2, 20)),
            dma((2, 5, 4)),
            dma((2, 4, 3)),
            dma((2, 4, 3)),
            dma((2, 4)),
            dma((2, 4)),
        ],
        compiler_params=pltpu.CompilerParams(
            collective_id=0, has_side_effects=True, vmem_limit_bytes=48 * 2**20
        ),
        cost_estimate=pl.CostEstimate(
            flops=4 * ROWS * width * PANEL,
            bytes_accessed=4 * ROWS * width,
            transcendentals=2 * ROWS * width,
        ),
    )(
        activations.reshape(ROWS, width),
        top_cotangent.reshape(ROWS, width),
        branch_gains.reshape(BLOCKS, 1, PANEL),
    )


def solution(mesh):
    in_specs = (P("section", None, "dp", None), P(None, "dp", None), P("section", None))
    out_specs = (P("section", "dp", None), P("section", "dp", None))
    return jax.shard_map(
        lambda *args: tuple(body(*args)),
        mesh=mesh,
        in_specs=in_specs,
        out_specs=out_specs,
        check_vma=False,
    )
```

```python
import jax
import jax.numpy as jnp
from jax import lax
from jax.experimental import pallas as pl
from jax.experimental.pallas import tpu as pltpu
from jax.sharding import PartitionSpec as P

PANEL = 384
ROWS = 224
BLOCKS = 16
SLAB = 32
SORTED = 112
JOBS = (0, 1, 2, 4, 3, 5, 6, 7)
RELAYED = (3, 6, 9, 10, 12, 14, 16, 16, 16)
MESH = pl.DeviceIdType.MESH
F32 = jnp.float32
BF16 = jnp.bfloat16


def gelu_slope(values):
    return (
        0.5 * (1.0 + lax.erf(values * 0.7071067811865476))
        + values * jnp.exp(-0.5 * values * values) * 0.3989422804014327
    )


def kernel(
    x_hbm,
    top_hbm,
    gains_hbm,
    in_out,
    grad_out,
    gains,
    whole,
    sorted_by_x,
    obuf,
    held,
    part,
    bsend,
    brecv,
    csend,
    crecv,
    fin,
    gain_load,
    x_load,
    c_in,
    relay_sent,
    a_sent,
    a_in,
    b_sent,
    b_in,
    c_sent,
    c_got,
):
    s = lax.axis_index("section")
    d = lax.axis_index("dp")
    core = s % 2
    zh, y, x = d // 16, (d // 4) % 4, d % 4
    a = jnp.where(core == 0, y, x)
    b = jnp.where(core == 0, x, y)

    def at(zz, aa, bb):
        return zz * 16 + jnp.where(core == 0, aa * 4 + bb, bb * 4 + aa)

    def peer_a(aa):
        return (s, at(zh, aa, b))

    def peer_b(bb):
        return (s, at(zh, a, bb))

    def owner(zz):
        return (s, at(zz, a, b))

    xbuf, cbuf = whole.at[0], whole.at[1]

    barrier = pltpu.get_barrier_semaphore()

    def greet(device):
        pl.semaphore_signal(barrier, inc=1, device_id=device, device_id_type=MESH)

    for o in (1, 2, 3):
        greet(peer_a((a + o) % 4))
        greet(peer_b((b + o) % 4))
        greet(owner((zh + o) % 4))

    @pl.when(s > 0)
    def _():
        greet((s - 1, d))

    @pl.when(s < 3)
    def _():
        greet((s + 1, d))

    first = 4 * (3 - zh) + (8 - x - y) % 4

    def block_at(p):
        i = jnp.where(p == 0, first, jnp.where(p <= first, p - 1, p))
        return ((zh + 1 + i // 4) % 4) * 4 + (i + x + y) % 4

    def columns(blk):
        return pl.ds(pl.multiple_of(blk * PANEL, PANEL), PANEL)

    def rows_of(aa):
        return pl.ds(pl.multiple_of(aa * ROWS, ROWS), ROWS)

    def load(p, _):
        blk = block_at(p)

        @pl.when(s > 0)
        def _():
            pltpu.make_async_copy(x_hbm.at[:, columns(blk)], xbuf.at[blk], x_load.at[blk]).start()

        @pl.when(s == 3)
        def _():
            pltpu.make_async_copy(top_hbm.at[:, columns(blk)], cbuf.at[blk], c_in.at[blk]).start()

        return 0

    lax.fori_loop(0, BLOCKS, load, 0)
    pltpu.make_async_copy(gains_hbm, gains, gain_load).start()

    others = 9 + jnp.where(s > 0, 1, 0) + jnp.where(s < 3, 1, 0)
    pl.semaphore_wait(barrier, others)

    def to_peer(f, src, slot, sent, aa):
        return pltpu.make_async_remote_copy(
            src_ref=src,
            dst_ref=held.at[f, slot, rows_of(a), :],
            send_sem=a_sent.at[f, sent],
            recv_sem=a_in.at[f, slot, a],
            device_id=peer_a(aa),
            device_id_type=MESH,
        )

    def keep(f, src, slot):
        return pltpu.make_async_copy(src, held.at[f, slot, rows_of(a), :], a_in.at[f, slot, a])

    def sends_block(zz, aa):
        return jnp.logical_or(core == 1, jnp.logical_or(zz != 0, aa != 0))

    def sort_and_send(f, j):
        zz = (zh + 1 + j) % 4

        def sort(i, _):
            rows = pl.ds(pl.multiple_of(i * SORTED, SORTED), SORTED)
            blocks = [whole[f, zz * 4 + yy, rows, :].astype(F32) for yy in range(4)]
            for xx in range(4):
                sorted_by_x[f, zz * 4 + xx, rows, :] = jnp.concatenate(
                    [block[:, xx * 96 : xx * 96 + 96] for block in blocks], axis=1
                ).astype(BF16)
            return 0

        lax.fori_loop(0, ROWS // SORTED, sort, 0)
        for o in (2, 1, 3):
            aa = (a + o) % 4
            to_peer(f, sorted_by_x.at[f, zz * 4 + aa], zz, zz * 4 + aa, aa).start()
        keep(f, sorted_by_x.at[f, zz * 4 + a], zz).start()

    panel_src = x_hbm.at[:, pl.ds(0, PANEL)]
    for o in (2, 1, 3):
        to_peer(0, panel_src, 4, 16 + o, (a + o) % 4).start()
    keep(0, panel_src, 4).start()

    def await_x(blk):
        pltpu.make_async_copy(xbuf.at[blk], xbuf.at[blk], x_load.at[blk]).wait()

    def send_x(j, _):
        zz = (zh + 1 + j) % 4

        @pl.when(core == 0)
        def _():
            for o in (2, 1, 3):
                aa = (a + o) % 4
                blk = zz * 4 + aa

                @pl.when(sends_block(zz, aa))
                def _():
                    to_peer(0, x_hbm.at[:, columns(blk)], zz, blk, aa).start()

            @pl.when(sends_block(zz, a))
            def _():
                keep(0, x_hbm.at[:, columns(zz * 4 + a)], zz).start()

        @pl.when(core == 1)
        def _():
            for yy in range(4):
                await_x(zz * 4 + yy)
            sort_and_send(0, j)

        return 0

    lax.fori_loop(0, 4, send_x, 0)
    pltpu.make_async_copy(gains_hbm, gains, gain_load).wait()

    def relay_copy(blk):
        return pltpu.make_async_remote_copy(
            src_ref=obuf.at[blk],
            dst_ref=cbuf.at[blk],
            send_sem=relay_sent.at[blk],
            recv_sem=c_in.at[blk],
            device_id=(s - 1, d),
            device_id_type=MESH,
        )

    def relay(p, _):
        blk = block_at(p)
        zz, q = blk // 4, blk % 4
        pltpu.make_async_copy(cbuf.at[blk], cbuf.at[blk], c_in.at[blk]).wait()

        @pl.when(p == 0)
        def _():
            for o in (2, 1, 3):
                to_peer(1, cbuf.at[blk], 4, 16 + o, (a + o) % 4).start()
            keep(1, cbuf.at[blk], 4).start()

        straight = jnp.logical_and(core == 0, p > 0)

        @pl.when(jnp.logical_and(straight, q != a))
        def _():
            to_peer(1, cbuf.at[blk], zz, blk, q).start()

        @pl.when(jnp.logical_and(straight, q == a))
        def _():
            keep(1, cbuf.at[blk], zz).start()

        @pl.when(s > 0)
        def _():
            @pl.when(core == 0)
            def _():
                await_x(blk)

            gain = gains[blk]

            def slab(i, _):
                rows = pl.ds(pl.multiple_of(i * SLAB, SLAB), SLAB)
                scaling = 1.0 + gain * gelu_slope(xbuf[blk, rows, :].astype(F32))
                obuf[blk, rows, :] = (cbuf[blk, rows, :].astype(F32) * scaling).astype(BF16)
                return 0

            lax.fori_loop(0, ROWS // SLAB, slab, 0)
            relay_copy(blk).start()

        early = first // 4
        ends = jnp.where(p % 4 == 3, p // 4 >= early, jnp.logical_and(p % 4 == 0, (p + 3) // 4 - 1 < early))

        @pl.when(jnp.logical_and(jnp.logical_and(core == 1, p > 0), ends))
        def _():
            sort_and_send(1, (p - 3) // 4)

        return 0

    def await_slot(f, slot):
        for aa in range(4):
            there = held.at[f, slot, pl.ds(aa * ROWS, ROWS), :]
            pltpu.make_async_copy(there, there, a_in.at[f, slot, aa]).wait()

    def b_copy(f, j, o):
        bb = (b + o) % 4
        return pltpu.make_async_remote_copy(
            src_ref=bsend.at[f, j, bb],
            dst_ref=brecv.at[f, j, o - 1],
            send_sem=b_sent.at[f, j, o - 1],
            recv_sem=b_in.at[f, j, o - 1],
            device_id=peer_b(bb),
            device_id_type=MESH,
        )

    def gram(f, j):
        zz = (zh + 1 + j) % 4
        slot = jnp.where(sends_block(zz, a), zz, 4)

        @pl.when(j == 0)
        def _():
            await_slot(f, 4)

        @pl.when(sends_block(zz, a))
        def _():
            await_slot(f, zz)

        part[f, j] = lax.dot_general(
            held[f, slot], held[f, 4], (((0,), (0,)), ((), ())), preferred_element_type=F32
        )
        for bb in range(4):
            bsend[f, j, bb] = part[f, j, pl.ds(bb * 96, 96), :].astype(BF16)
        for o in (2, 1, 3):
            b_copy(f, j, o).start()

    def c_copy(f, j):
        return pltpu.make_async_remote_copy(
            src_ref=csend.at[f, j],
            dst_ref=crecv.at[f, j],
            send_sem=c_sent.at[f, j],
            recv_sem=c_got.at[f, j],
            device_id=owner((zh + 1 + j) % 4),
            device_id_type=MESH,
        )

    def sum_b(f, j):
        total = part[f, j, pl.ds(pl.multiple_of(b * 96, 96), 96), :]
        for o in (1, 3, 2):
            b_copy(f, j, o).wait_recv()
            total = total + brecv[f, j, o - 1].astype(F32)

        @pl.when(j == 3)
        def _():
            fin[f] = total

        @pl.when(j < 3)
        def _():
            csend[f, j] = total.astype(BF16)
            c_copy(f, j).start()

    def finish(f, out):
        total = fin[f]
        for j in range(3):
            c_copy(f, j).wait_recv()
            total = total + crecv[f, j].astype(F32)
        out[...] = total

    upper = s >= 2

    def pick(table, t):
        value = jnp.int32(table[-1])
        for i in range(len(table) - 1):
            value = jnp.where(t == i, table[i], value)
        return value

    def job_at(t):
        return jnp.where(upper, t, pick(JOBS, t))

    def relayed_by(t):
        return jnp.where(upper, BLOCKS, pick(RELAYED, t))

    def step(t, done):
        upto = relayed_by(t)
        lax.fori_loop(done, upto, relay, 0)

        @pl.when(t < 8)
        def _():
            job = job_at(t)
            gram(job // 4, job % 4)

        @pl.when(t > 0)
        def _():
            job = job_at(t - 1)
            sum_b(job // 4, job % 4)

        return upto

    lax.fori_loop(0, 9, step, jnp.int32(0))
    finish(0, in_out)
    finish(1, grad_out)

    for f in range(2):
        for o in (1, 2, 3):
            to_peer(f, cbuf.at[0], 4, 16 + o, (a + o) % 4).wait_send()

        def sent(blk, _):
            q = blk % 4

            @pl.when(jnp.logical_and(sends_block(blk // 4, q), q != a))
            def _():
                to_peer(f, cbuf.at[blk], blk // 4, blk, q).wait_send()

            return 0

        lax.fori_loop(0, BLOCKS, sent, 0)
        for j in range(4):
            for o in (1, 2, 3):
                b_copy(f, j, o).wait_send()
        for j in range(3):
            c_copy(f, j).wait_send()

    @pl.when(s > 0)
    def _():
        def relayed(blk, _):
            relay_copy(blk).wait_send()
            return 0

        lax.fori_loop(0, BLOCKS, relayed, 0)


def body(activations, top_cotangent, branch_gains):
    width = activations.shape[-1]
    total_rows = ROWS * lax.axis_size("dp")
    dma = pltpu.SemaphoreType.DMA
    sums = pl.pallas_call(
        kernel,
        out_shape=[jax.ShapeDtypeStruct((96, PANEL), F32)] * 2,
        in_specs=[
            pl.BlockSpec(memory_space=pl.ANY),
            pl.BlockSpec(memory_space=pl.ANY),
            pl.BlockSpec(memory_space=pl.ANY),
        ],
        out_specs=[pl.BlockSpec(memory_space=pltpu.VMEM)] * 2,
        scratch_shapes=[
            pltpu.VMEM((BLOCKS, 1, PANEL), F32),
            pltpu.VMEM((2, BLOCKS, ROWS, PANEL), BF16),
            pltpu.VMEM((2, BLOCKS, ROWS, PANEL), BF16),
            pltpu.VMEM((BLOCKS, ROWS, PANEL), BF16),
            pltpu.VMEM((2, 5, 4 * ROWS, PANEL), BF16),
            pltpu.VMEM((2, 4, PANEL, PANEL), F32),
            pltpu.VMEM((2, 4, 4, 96, PANEL), BF16),
            pltpu.VMEM((2, 4, 3, 96, PANEL), BF16),
            pltpu.VMEM((2, 3, 96, PANEL), BF16),
            pltpu.VMEM((2, 3, 96, PANEL), BF16),
            pltpu.VMEM((2, 96, PANEL), F32),
            dma,
            dma((BLOCKS,)),
            dma((BLOCKS,)),
            dma((BLOCKS,)),
            dma((2, 20)),
            dma((2, 5, 4)),
            dma((2, 4, 3)),
            dma((2, 4, 3)),
            dma((2, 3)),
            dma((2, 3)),
        ],
        compiler_params=pltpu.CompilerParams(
            collective_id=0, has_side_effects=True, vmem_limit_bytes=56 * 2**20
        ),
        cost_estimate=pl.CostEstimate(
            flops=4 * ROWS * width * PANEL,
            bytes_accessed=4 * ROWS * width,
            transcendentals=2 * ROWS * width,
        ),
    )(
        activations.reshape(ROWS, width),
        top_cotangent.reshape(ROWS, width),
        branch_gains.reshape(BLOCKS, 1, PANEL),
    )
    return tuple((total / F32(total_rows))[None] for total in sums)


def solution(mesh):
    in_specs = (P("section", None, "dp", None), P(None, "dp", None), P("section", None))
    out_specs = (P("section", "dp", None), P("section", "dp", None))
    return jax.shard_map(
        body,
        mesh=mesh,
        in_specs=in_specs,
        out_specs=out_specs,
        check_vma=False,
    )
```

```python
import jax
import jax.numpy as jnp
from jax import lax
from jax.experimental import pallas as pl
from jax.experimental.pallas import tpu as pltpu
from jax.sharding import PartitionSpec as P

PANEL = 384
ROWS = 224
BLOCKS = 16
SLAB = 32
SORTED = 112
KINDS = RELAY, HAND_C, GRAM_X, GRAM_C, SUM_A, SUM_B, MEET, SWAP_X = range(8)
R, S, G, D, A, B, M, X = (32 * kind for kind in KINDS)
SECTION3 = (R + 2, X + 0, R + 4, X + 1, R + 6, X + 2, R + 8, X + 3, R + 16, G + 0, G + 1, S + 0, S + 1, G + 2, G + 3, S + 2, S + 3, A + 0, A + 1, A + 2, A + 3, D + 0, D + 1, M + 0, B + 0, B + 1, B + 2, B + 3, D + 2, D + 3, B + 4, B + 5, B + 6, B + 7)
SECTION2 = (X + 0, X + 1, X + 2, X + 3, R + 16, G + 0, G + 1, S + 0, S + 1, G + 2, G + 3, S + 2, S + 3, A + 0, A + 1, A + 2, A + 3, D + 0, D + 1, M + 0, B + 0, B + 1, B + 2, B + 3, D + 2, D + 3, B + 4, B + 5, B + 6, B + 7)
SECTION1 = (X + 0, X + 1, X + 2, X + 3, R + 4, G + 0, G + 1, R + 5, S + 0, G + 2, G + 3, R + 9, S + 1, A + 0, A + 1, D + 0, R + 10, A + 2, A + 3, R + 13, S + 2, D + 1, M + 0, B + 0, B + 1, B + 4, R + 16, S + 3, B + 2, B + 3, D + 2, B + 5, D + 3, B + 6, B + 7)
SECTION0 = (X + 0, X + 1, X + 2, X + 3, R + 4, G + 0, G + 1, R + 5, S + 0, G + 2, G + 3, R + 9, S + 1, A + 0, A + 1, D + 0, R + 10, A + 2, A + 3, R + 13, S + 2, D + 1, M + 0, B + 0, B + 1, B + 4, R + 16, S + 3, B + 2, B + 3, D + 2, B + 5, D + 3, B + 6, B + 7)
WORDS = 15
MESH = pl.DeviceIdType.MESH
F32 = jnp.float32
BF16 = jnp.bfloat16


def packed(ops):
    codes = ops + (R + BLOCKS,) * (3 * WORDS - len(ops))
    return [codes[i] + 256 * codes[i + 1] + 65536 * codes[i + 2] for i in range(0, len(codes), 3)]


def gelu_slope(values):
    return (
        0.5 * (1.0 + lax.erf(values * 0.7071067811865476))
        + values * jnp.exp(-0.5 * values * values) * 0.3989422804014327
    )


def kernel(
    x_hbm,
    top_hbm,
    gains_hbm,
    in_out,
    grad_out,
    gains,
    whole,
    sorted_by_x,
    obuf,
    held,
    gathered,
    part,
    asend,
    arecv,
    bsend,
    brecv,
    csend,
    crecv,
    fin,
    gain_load,
    x_load,
    c_in,
    relay_sent,
    swap_sent,
    swap_in,
    gather_sent,
    gather_in,
    a_sent,
    a_in,
    b_sent,
    b_in,
    c_sent,
    c_got,
    above,
):
    s = lax.axis_index("section")
    d = lax.axis_index("dp")
    core = s % 2
    zh, y, x = d // 16, (d // 4) % 4, d % 4
    a = jnp.where(core == 0, y, x)
    b = jnp.where(core == 0, x, y)
    xbuf, cbuf = whole.at[0], whole.at[1]

    def at(zz, aa, bb):
        return zz * 16 + jnp.where(core == 0, aa * 4 + bb, bb * 4 + aa)

    def peer_a(aa):
        return (s, at(zh, aa, b))

    def peer_b(bb):
        return (s, at(zh, a, bb))

    def owner(zz):
        return (s, at(zz, a, b))

    flip, mirror = a + 1 - 2 * (a % 2), 3 - a
    opposite = (a + 2) % 4

    def first_of(j):
        return jnp.where(j % 2 == 0, flip, mirror)

    def second_of(j):
        return jnp.where(j % 2 == 0, mirror, flip)

    barrier = pltpu.get_barrier_semaphore()

    def greet(device):
        pl.semaphore_signal(barrier, inc=1, device_id=device, device_id_type=MESH)

    greet(peer_a(flip))
    greet(peer_a(mirror))
    greet(peer_a(opposite))
    for o in (1, 2, 3):
        greet(peer_b((b + o) % 4))

        @pl.when(zh + o < 4)
        def _():
            greet(owner(zh + o))

    @pl.when(s > 0)
    def _():
        greet((s - 1, d))

    @pl.when(s < 3)
    def _():
        greet((s + 1, d))

    def part_at(j):
        return jnp.where(j == 3, zh, jnp.where(j < zh, j, j + 1))

    panel_part = jnp.where(zh == 0, 3, 0)
    first = 4 * panel_part + (8 - x - y) % 4

    def block_at(p):
        i = jnp.where(p == 0, first, jnp.where(p <= first, p - 1, p))
        return part_at(i // 4) * 4 + (i + x + y) % 4

    def columns(blk):
        return pl.ds(pl.multiple_of(blk * PANEL, PANEL), PANEL)

    def load(p, _):
        blk = block_at(p)

        @pl.when(s > 0)
        def _():
            pltpu.make_async_copy(x_hbm.at[:, columns(blk)], xbuf.at[blk], x_load).start()

        @pl.when(s == 3)
        def _():
            pltpu.make_async_copy(top_hbm.at[:, columns(blk)], cbuf.at[blk], c_in.at[blk]).start()

        return 0

    lax.fori_loop(0, BLOCKS, load, 0)
    pltpu.make_async_copy(gains_hbm, gains, gain_load).start()

    others = 6 + zh + jnp.where(s > 0, 1, 0) + jnp.where(s < 3, 1, 0)
    pl.semaphore_wait(barrier, others)

    for o in (1, 2, 3):

        @pl.when(zh >= o)
        def _():
            pl.semaphore_signal(above, inc=1, device_id=owner(zh - o), device_id_type=MESH)


    def swap(src, slot, aa):
        return pltpu.make_async_remote_copy(
            src_ref=src,
            dst_ref=held.at[slot, pl.ds(ROWS, ROWS), :],
            send_sem=swap_sent,
            recv_sem=swap_in.at[slot],
            device_id=peer_a(aa),
            device_id_type=MESH,
        )

    def keep(src, slot):
        return pltpu.make_async_copy(src, held.at[slot, pl.ds(0, ROWS), :], swap_in.at[slot])

    def is_panel(zz, q):
        return jnp.logical_and(core == 0, jnp.logical_and(zz == 0, q == 0))

    def other_than_panel(zz, q):
        return jnp.logical_not(is_panel(zz, q))

    def swap_part(j, piece):
        zz = part_at(j)
        to = first_of(j)
        for q, slot in ((opposite, 2 * j + 1), (to, 2 * j)):

            @pl.when(other_than_panel(zz, q))
            def _():
                swap(piece(zz * 4 + q), slot, to).start()

        for q, slot in ((second_of(j), 2 * j + 1), (a, 2 * j)):

            @pl.when(other_than_panel(zz, q))
            def _():
                keep(piece(zz * 4 + q), slot).start()

    def rows_of(aa):
        return pl.ds(pl.multiple_of(aa * ROWS, ROWS), ROWS)

    def hand(src, slot, aa):
        return pltpu.make_async_remote_copy(
            src_ref=src,
            dst_ref=gathered.at[slot, rows_of(a), :],
            send_sem=gather_sent,
            recv_sem=gather_in.at[slot],
            device_id=peer_a(aa),
            device_id_type=MESH,
        )

    def hold(src, slot):
        return pltpu.make_async_copy(src, gathered.at[slot, rows_of(a), :], gather_in.at[slot])

    def hand_part(j, piece):
        zz = part_at(j)
        for o in (2, 1, 3):
            aa = (a + o) % 4

            @pl.when(other_than_panel(zz, aa))
            def _():
                hand(piece(zz * 4 + aa), j, aa).start()

        @pl.when(other_than_panel(zz, a))
        def _():
            hold(piece(zz * 4 + a), j).start()

    def sort_part(f, j):
        zz = part_at(j)

        def sort(i, _):
            rows = pl.ds(pl.multiple_of(i * SORTED, SORTED), SORTED)
            blocks = [whole[f, zz * 4 + yy, rows, :].astype(F32) for yy in range(4)]
            for xx in range(4):
                sorted_by_x[f, zz * 4 + xx, rows, :] = jnp.concatenate(
                    [block[:, xx * 96 : xx * 96 + 96] for block in blocks], axis=1
                ).astype(BF16)
            return 0

        lax.fori_loop(0, ROWS // SORTED, sort, 0)

    x_panel = x_hbm.at[:, pl.ds(0, PANEL)]
    swap(x_panel, 8, flip).start()
    swap(x_panel, 9, mirror).start()
    keep(x_panel, 8).start()
    keep(x_panel, 9).start()

    def swap_x(j):
        @pl.when(core == 0)
        def _():
            swap_part(j, lambda blk: x_hbm.at[:, columns(blk)])

        @pl.when(core == 1)
        def _():
            sort_part(0, j)
            swap_part(j, lambda blk: sorted_by_x.at[0, blk])

    @pl.when(s > 0)
    def _():
        pltpu.make_async_copy(xbuf, xbuf, x_load).wait()

    pltpu.make_async_copy(gains_hbm, gains, gain_load).wait()

    def relay_copy(blk):
        return pltpu.make_async_remote_copy(
            src_ref=obuf.at[blk],
            dst_ref=cbuf.at[blk],
            send_sem=relay_sent,
            recv_sem=c_in.at[blk],
            device_id=(s - 1, d),
            device_id_type=MESH,
        )

    def relay(p, _):
        blk = block_at(p)
        pltpu.make_async_copy(cbuf.at[blk], cbuf.at[blk], c_in.at[blk]).wait()

        @pl.when(p == 0)
        def _():
            for o in (2, 1, 3):
                hand(cbuf.at[blk], 4, (a + o) % 4).start()
            hold(cbuf.at[blk], 4).start()

        @pl.when(s > 0)
        def _():
            gain = gains[blk]

            def slab(i, _):
                rows = pl.ds(pl.multiple_of(i * SLAB, SLAB), SLAB)
                scaling = 1.0 + gain * gelu_slope(xbuf[blk, rows, :].astype(F32))
                obuf[blk, rows, :] = (cbuf[blk, rows, :].astype(F32) * scaling).astype(BF16)
                return 0

            lax.fori_loop(0, ROWS // SLAB, slab, 0)
            relay_copy(blk).start()

        return 0

    def hand_c(j):
        @pl.when(core == 0)
        def _():
            hand_part(j, lambda blk: cbuf.at[blk])

        @pl.when(core == 1)
        def _():
            sort_part(1, j)
            hand_part(j, lambda blk: sorted_by_x.at[1, blk])

    def await_swap(slot):
        pltpu.make_async_copy(held.at[slot], held.at[slot], swap_in.at[slot]).wait()

    def await_gather(slot):
        pltpu.make_async_copy(gathered.at[slot], gathered.at[slot], gather_in.at[slot]).wait()

    def product(left, right):
        return lax.dot_general(left, right, (((0,), (0,)), ((), ())), preferred_element_type=F32)

    def a_copy(j):
        return pltpu.make_async_remote_copy(
            src_ref=asend.at[j],
            dst_ref=arecv.at[j],
            send_sem=a_sent,
            recv_sem=a_in.at[j],
            device_id=peer_a(second_of(j)),
            device_id_type=MESH,
        )

    def gram_x(j):
        zz = part_at(j)
        panel = 8 + j % 2

        @pl.when(j < 2)
        def _():
            await_swap(panel)

        def piece(q, slot):
            @pl.when(other_than_panel(zz, q))
            def _():
                await_swap(slot)

            return product(held[jnp.where(is_panel(zz, q), panel, slot)], held[panel])

        asend[j] = piece(second_of(j), 2 * j + 1).astype(BF16)
        a_copy(j).start()
        part[0, j] = piece(a, 2 * j)

    def gram_c(j):
        zz = part_at(j)

        @pl.when(j == 0)
        def _():
            await_gather(4)

        @pl.when(other_than_panel(zz, a))
        def _():
            await_gather(j)

        part[1, j] = product(gathered[jnp.where(is_panel(zz, a), 4, j)], gathered[4])
        for bb in range(4):
            bsend[1, j, bb] = part[1, j, pl.ds(bb * 96, 96), :].astype(BF16)
        for o in (2, 1, 3):
            b_copy(1, j, o).start()

    def b_copy(f, j, o):
        bb = (b + o) % 4
        return pltpu.make_async_remote_copy(
            src_ref=bsend.at[f, j, bb],
            dst_ref=brecv.at[f, j, o - 1],
            send_sem=b_sent.at[f],
            recv_sem=b_in.at[f, j],
            device_id=peer_b(bb),
            device_id_type=MESH,
        )

    def sum_a(j):
        a_copy(j).wait_recv()
        for bb in range(4):
            rows = pl.ds(bb * 96, 96)
            total = part[0, j, rows, :] + arecv[j, rows, :].astype(F32)
            part[0, j, rows, :] = total
            bsend[0, j, bb] = total.astype(BF16)
        for o in (2, 1, 3):
            b_copy(0, j, o).start()

    def c_copy(f, j):
        zz = part_at(j)
        return pltpu.make_async_remote_copy(
            src_ref=csend.at[f, j],
            dst_ref=crecv.at[f, jnp.where(zh < zz, zh, zh - 1)],
            send_sem=c_sent.at[f],
            recv_sem=c_got.at[f],
            device_id=owner(zz),
            device_id_type=MESH,
        )

    def meet_above():
        @pl.when(zh < 3)
        def _():
            pl.semaphore_wait(above, 3 - zh)

    def sum_b(f, j):
        pltpu.make_async_copy(brecv.at[f, j], brecv.at[f, j], b_in.at[f, j]).wait()
        total = part[f, j, pl.ds(pl.multiple_of(b * 96, 96), 96), :]
        for o in (1, 3, 2):
            total = total + brecv[f, j, o - 1].astype(F32)

        @pl.when(j == 3)
        def _():
            fin[f] = total

        @pl.when(j < 3)
        def _():
            csend[f, j] = total.astype(BF16)
            c_copy(f, j).start()

    def finish(f, out):
        pltpu.make_async_copy(crecv.at[f], crecv.at[f], c_got.at[f]).wait()
        total = fin[f]
        for j in range(3):
            total = total + crecv[f, j].astype(F32)
        out[...] = total

    words = [
        jnp.where(s == 0, w0, jnp.where(s == 1, w1, jnp.where(s == 2, w2, w3)))
        for w0, w1, w2, w3 in zip(*map(packed, (SECTION0, SECTION1, SECTION2, SECTION3)))
    ]

    def step(t, done):
        word = words[-1]
        for i in range(len(words) - 1):
            word = jnp.where(t // 3 == i, words[i], word)
        op = jnp.where(t % 3 == 0, word, jnp.where(t % 3 == 1, word // 256, word // 65536)) % 256
        kind, what = op // 32, op % 32
        upto = jnp.where(kind == RELAY, what, done)
        lax.fori_loop(done, upto, relay, 0)

        @pl.when(kind == HAND_C)
        def _():
            hand_c(what)

        @pl.when(kind == SWAP_X)
        def _():
            swap_x(what)

        @pl.when(kind == GRAM_X)
        def _():
            gram_x(what)

        @pl.when(kind == GRAM_C)
        def _():
            gram_c(what)

        @pl.when(kind == SUM_A)
        def _():
            sum_a(what)

        @pl.when(kind == MEET)
        def _():
            meet_above()

        @pl.when(kind == SUM_B)
        def _():
            sum_b(what // 4, what % 4)

        return upto

    lax.fori_loop(0, 3 * len(words), step, jnp.int32(0))
    finish(0, in_out)
    finish(1, grad_out)

    def await_sent(ref, sem):
        pltpu.make_async_copy(ref, ref, sem).wait()

    swaps = jnp.logical_and(core == 0, jnp.logical_and(a != 0, second_of(panel_part) != 0))
    hands = jnp.logical_and(core == 0, a != 0)
    for less, count, sem in ((swaps, 10, swap_sent), (hands, 15, gather_sent)):

        @pl.when(less)
        def _():
            await_sent(xbuf.at[pl.ds(0, count - 1)], sem)

        @pl.when(jnp.logical_not(less))
        def _():
            await_sent(xbuf.at[pl.ds(0, count)], sem)

    await_sent(asend, a_sent)
    for f in range(2):
        await_sent(bsend.at[f, pl.ds(0, 3)], b_sent.at[f])
        await_sent(csend.at[f], c_sent.at[f])

    @pl.when(s > 0)
    def _():
        await_sent(obuf, relay_sent)


def body(activations, top_cotangent, branch_gains):
    width = activations.shape[-1]
    total_rows = ROWS * lax.axis_size("dp")
    dma = pltpu.SemaphoreType.DMA
    sums = pl.pallas_call(
        kernel,
        out_shape=[jax.ShapeDtypeStruct((96, PANEL), F32)] * 2,
        in_specs=[
            pl.BlockSpec(memory_space=pl.ANY),
            pl.BlockSpec(memory_space=pl.ANY),
            pl.BlockSpec(memory_space=pl.ANY),
        ],
        out_specs=[pl.BlockSpec(memory_space=pltpu.VMEM)] * 2,
        scratch_shapes=[
            pltpu.VMEM((BLOCKS, 1, PANEL), F32),
            pltpu.VMEM((2, BLOCKS, ROWS, PANEL), BF16),
            pltpu.VMEM((2, BLOCKS, ROWS, PANEL), BF16),
            pltpu.VMEM((BLOCKS, ROWS, PANEL), BF16),
            pltpu.VMEM((10, 2 * ROWS, PANEL), BF16),
            pltpu.VMEM((5, 4 * ROWS, PANEL), BF16),
            pltpu.VMEM((2, 4, PANEL, PANEL), F32),
            pltpu.VMEM((4, PANEL, PANEL), BF16),
            pltpu.VMEM((4, PANEL, PANEL), BF16),
            pltpu.VMEM((2, 4, 4, 96, PANEL), BF16),
            pltpu.VMEM((2, 4, 3, 96, PANEL), BF16),
            pltpu.VMEM((2, 3, 96, PANEL), BF16),
            pltpu.VMEM((2, 3, 96, PANEL), BF16),
            pltpu.VMEM((2, 96, PANEL), F32),
            dma,
            dma,
            dma((BLOCKS,)),
            dma,
            dma,
            dma((10,)),
            dma,
            dma((5,)),
            dma,
            dma((4,)),
            dma((2,)),
            dma((2, 4)),
            dma((2,)),
            dma((2,)),
            pltpu.SemaphoreType.REGULAR,
        ],
        compiler_params=pltpu.CompilerParams(
            collective_id=0, has_side_effects=True, vmem_limit_bytes=56 * 2**20
        ),
        cost_estimate=pl.CostEstimate(
            flops=4 * ROWS * width * PANEL,
            bytes_accessed=4 * ROWS * width,
            transcendentals=2 * ROWS * width,
        ),
    )(
        activations.reshape(ROWS, width),
        top_cotangent.reshape(ROWS, width),
        branch_gains.reshape(BLOCKS, 1, PANEL),
    )
    return tuple((total / F32(total_rows))[None] for total in sums)


def solution(mesh):
    in_specs = (P("section", None, "dp", None), P(None, "dp", None), P("section", None))
    out_specs = (P("section", "dp", None), P("section", "dp", None))
    return jax.shard_map(
        body,
        mesh=mesh,
        in_specs=in_specs,
        out_specs=out_specs,
        check_vma=False,
    )
```

```python
import jax
import jax.numpy as jnp
from jax import lax
from jax.experimental import pallas as pl
from jax.experimental.pallas import tpu as pltpu
from jax.sharding import PartitionSpec as P

PANEL = 384
ROWS = 224
BLOCKS = 16
SLAB = 32
SORTED = 112
KINDS = RELAY, HAND_C, GRAM_X, GRAM_C, SUM_A, SUM_B, MEET, SWAP_X = range(8)
R, S, G, D, A, B, M, X = (32 * kind for kind in KINDS)
SECTION3 = (R + 2, X + 0, R + 4, X + 1, R + 6, X + 2, R + 8, X + 3, R + 16, G + 0, G + 1, G + 2, G + 3, S + 0, S + 1, A + 0, A + 1, A + 2, A + 3, S + 2, D + 0, S + 3, D + 1, M + 0, B + 0, B + 1, B + 2, B + 3, B + 4, D + 2, B + 5, D + 3, B + 6, B + 7)
SECTION2 = (X + 0, X + 1, X + 2, X + 3, R + 16, G + 0, G + 1, G + 2, G + 3, S + 0, S + 1, A + 0, A + 1, A + 2, A + 3, S + 2, D + 0, S + 3, D + 1, M + 0, B + 0, B + 1, B + 2, B + 3, B + 4, D + 2, B + 5, D + 3, B + 6, B + 7)
SECTION1 = (X + 0, X + 1, X + 2, X + 3, R + 4, G + 0, G + 1, R + 5, S + 0, G + 2, G + 3, R + 9, S + 1, A + 0, R + 10, A + 1, D + 0, A + 2, A + 3, R + 13, S + 2, D + 1, M + 0, B + 0, B + 1, B + 4, R + 16, S + 3, B + 2, B + 3, D + 2, B + 5, D + 3, B + 6, B + 7)
SECTION0 = (X + 0, X + 1, X + 2, X + 3, R + 4, G + 0, G + 1, R + 5, S + 0, G + 2, G + 3, R + 9, S + 1, A + 0, R + 10, A + 1, D + 0, A + 2, A + 3, R + 13, S + 2, D + 1, M + 0, B + 0, B + 1, B + 4, R + 16, S + 3, B + 2, B + 3, D + 2, B + 5, D + 3, B + 6, B + 7)
WORDS = 15
MESH = pl.DeviceIdType.MESH
F32 = jnp.float32
BF16 = jnp.bfloat16


def packed(ops):
    codes = ops + (R + BLOCKS,) * (3 * WORDS - len(ops))
    return [codes[i] + 256 * codes[i + 1] + 65536 * codes[i + 2] for i in range(0, len(codes), 3)]


def gelu_slope(values):
    return (
        0.5 * (1.0 + lax.erf(values * 0.7071067811865476))
        + values * jnp.exp(-0.5 * values * values) * 0.3989422804014327
    )


def kernel(
    x_hbm,
    top_hbm,
    gains_hbm,
    in_out,
    grad_out,
    gains,
    whole,
    sorted_by_x,
    obuf,
    held,
    gathered,
    part,
    asend,
    arecv,
    bsend,
    brecv,
    csend,
    crecv,
    fin,
    gain_load,
    x_load,
    c_in,
    relay_sent,
    swap_sent,
    swap_in,
    gather_sent,
    gather_in,
    a_sent,
    a_in,
    b_sent,
    b_in,
    c_sent,
    c_got,
    above,
):
    s = lax.axis_index("section")
    d = lax.axis_index("dp")
    core = s % 2
    zh, y, x = d // 16, (d // 4) % 4, d % 4
    a = jnp.where(core == 0, y, x)
    b = jnp.where(core == 0, x, y)
    xbuf, cbuf = whole.at[0], whole.at[1]

    def at(zz, aa, bb):
        return zz * 16 + jnp.where(core == 0, aa * 4 + bb, bb * 4 + aa)

    def peer_a(aa):
        return (s, at(zh, aa, b))

    def peer_b(bb):
        return (s, at(zh, a, bb))

    def owner(zz):
        return (s, at(zz, a, b))

    flip, mirror = a + 1 - 2 * (a % 2), 3 - a
    opposite = (a + 2) % 4

    def first_of(j):
        return jnp.where(j % 2 == 0, flip, mirror)

    def second_of(j):
        return jnp.where(j % 2 == 0, mirror, flip)

    barrier = pltpu.get_barrier_semaphore()

    def greet(device):
        pl.semaphore_signal(barrier, inc=1, device_id=device, device_id_type=MESH)

    greet(peer_a(flip))
    greet(peer_a(mirror))
    greet(peer_a(opposite))
    for o in (1, 2, 3):
        greet(peer_b((b + o) % 4))

        @pl.when(zh + o < 4)
        def _():
            greet(owner(zh + o))

    @pl.when(s > 0)
    def _():
        greet((s - 1, d))

    @pl.when(s < 3)
    def _():
        greet((s + 1, d))

    def part_at(j):
        return jnp.where(j == 3, zh, jnp.where(j < zh, j, j + 1))

    panel_part = jnp.where(zh == 0, 3, 0)
    first = 4 * panel_part + (8 - x - y) % 4

    def block_at(p):
        i = jnp.where(p == 0, first, jnp.where(p <= first, p - 1, p))
        return part_at(i // 4) * 4 + (i + x + y) % 4

    def columns(blk):
        return pl.ds(pl.multiple_of(blk * PANEL, PANEL), PANEL)

    def load(p, _):
        blk = block_at(p)

        @pl.when(s > 0)
        def _():
            pltpu.make_async_copy(x_hbm.at[:, columns(blk)], xbuf.at[blk], x_load).start()

        @pl.when(s == 3)
        def _():
            pltpu.make_async_copy(top_hbm.at[:, columns(blk)], cbuf.at[blk], c_in.at[blk]).start()

        return 0

    lax.fori_loop(0, BLOCKS, load, 0)
    pltpu.make_async_copy(gains_hbm, gains, gain_load).start()

    others = 6 + zh + jnp.where(s > 0, 1, 0) + jnp.where(s < 3, 1, 0)
    pl.semaphore_wait(barrier, others)

    for o in (1, 2, 3):

        @pl.when(zh >= o)
        def _():
            pl.semaphore_signal(above, inc=1, device_id=owner(zh - o), device_id_type=MESH)


    def swap(src, slot, aa):
        return pltpu.make_async_remote_copy(
            src_ref=src,
            dst_ref=held.at[slot, pl.ds(ROWS, ROWS), :],
            send_sem=swap_sent,
            recv_sem=swap_in.at[slot],
            device_id=peer_a(aa),
            device_id_type=MESH,
        )

    def keep(src, slot):
        return pltpu.make_async_copy(src, held.at[slot, pl.ds(0, ROWS), :], swap_in.at[slot])

    def is_panel(zz, q):
        return jnp.logical_and(core == 0, jnp.logical_and(zz == 0, q == 0))

    def other_than_panel(zz, q):
        return jnp.logical_not(is_panel(zz, q))

    def swap_part(j, piece):
        zz = part_at(j)
        to = first_of(j)
        for q, slot in ((opposite, 2 * j + 1), (to, 2 * j)):

            @pl.when(other_than_panel(zz, q))
            def _():
                swap(piece(zz * 4 + q), slot, to).start()

        for q, slot in ((second_of(j), 2 * j + 1), (a, 2 * j)):

            @pl.when(other_than_panel(zz, q))
            def _():
                keep(piece(zz * 4 + q), slot).start()

    def rows_of(aa):
        return pl.ds(pl.multiple_of(aa * ROWS, ROWS), ROWS)

    def hand(src, slot, aa):
        return pltpu.make_async_remote_copy(
            src_ref=src,
            dst_ref=gathered.at[slot, rows_of(a), :],
            send_sem=gather_sent,
            recv_sem=gather_in.at[slot],
            device_id=peer_a(aa),
            device_id_type=MESH,
        )

    def hold(src, slot):
        return pltpu.make_async_copy(src, gathered.at[slot, rows_of(a), :], gather_in.at[slot])

    def hand_part(j, piece):
        zz = part_at(j)
        for o in (2, 1, 3):
            aa = (a + o) % 4

            @pl.when(other_than_panel(zz, aa))
            def _():
                hand(piece(zz * 4 + aa), j, aa).start()

        @pl.when(other_than_panel(zz, a))
        def _():
            hold(piece(zz * 4 + a), j).start()

    def sort_part(f, j):
        zz = part_at(j)

        def sort(i, _):
            rows = pl.ds(pl.multiple_of(i * SORTED, SORTED), SORTED)
            blocks = [whole[f, zz * 4 + yy, rows, :].astype(F32) for yy in range(4)]
            for xx in range(4):
                sorted_by_x[f, zz * 4 + xx, rows, :] = jnp.concatenate(
                    [block[:, xx * 96 : xx * 96 + 96] for block in blocks], axis=1
                ).astype(BF16)
            return 0

        lax.fori_loop(0, ROWS // SORTED, sort, 0)

    x_panel = x_hbm.at[:, pl.ds(0, PANEL)]
    swap(x_panel, 8, flip).start()
    swap(x_panel, 9, mirror).start()
    keep(x_panel, 8).start()
    keep(x_panel, 9).start()

    def swap_x(j):
        @pl.when(core == 0)
        def _():
            swap_part(j, lambda blk: x_hbm.at[:, columns(blk)])

        @pl.when(core == 1)
        def _():
            sort_part(0, j)
            swap_part(j, lambda blk: sorted_by_x.at[0, blk])

    @pl.when(s > 0)
    def _():
        pltpu.make_async_copy(xbuf, xbuf, x_load).wait()

    pltpu.make_async_copy(gains_hbm, gains, gain_load).wait()

    def relay_copy(blk):
        return pltpu.make_async_remote_copy(
            src_ref=obuf.at[blk],
            dst_ref=cbuf.at[blk],
            send_sem=relay_sent,
            recv_sem=c_in.at[blk],
            device_id=(s - 1, d),
            device_id_type=MESH,
        )

    def relay(p, _):
        blk = block_at(p)
        pltpu.make_async_copy(cbuf.at[blk], cbuf.at[blk], c_in.at[blk]).wait()

        @pl.when(p == 0)
        def _():
            for o in (2, 1, 3):
                hand(cbuf.at[blk], 4, (a + o) % 4).start()
            hold(cbuf.at[blk], 4).start()

        @pl.when(s > 0)
        def _():
            gain = gains[blk]

            def slab(i, _):
                rows = pl.ds(pl.multiple_of(i * SLAB, SLAB), SLAB)
                scaling = 1.0 + gain * gelu_slope(xbuf[blk, rows, :].astype(F32))
                obuf[blk, rows, :] = (cbuf[blk, rows, :].astype(F32) * scaling).astype(BF16)
                return 0

            lax.fori_loop(0, ROWS // SLAB, slab, 0)
            relay_copy(blk).start()

        return 0

    def hand_c(j):
        @pl.when(core == 0)
        def _():
            hand_part(j, lambda blk: cbuf.at[blk])

        @pl.when(core == 1)
        def _():
            sort_part(1, j)
            hand_part(j, lambda blk: sorted_by_x.at[1, blk])

    def await_swap(slot):
        pltpu.make_async_copy(held.at[slot], held.at[slot], swap_in.at[slot]).wait()

    def await_gather(slot):
        pltpu.make_async_copy(gathered.at[slot], gathered.at[slot], gather_in.at[slot]).wait()

    def product(left, right):
        return lax.dot_general(left, right, (((0,), (0,)), ((), ())), preferred_element_type=F32)

    def a_copy(j):
        return pltpu.make_async_remote_copy(
            src_ref=asend.at[j],
            dst_ref=arecv.at[j],
            send_sem=a_sent,
            recv_sem=a_in.at[j],
            device_id=peer_a(second_of(j)),
            device_id_type=MESH,
        )

    def gram_x(j):
        zz = part_at(j)
        panel = 8 + j % 2

        @pl.when(j < 2)
        def _():
            await_swap(panel)

        def piece(q, slot):
            @pl.when(other_than_panel(zz, q))
            def _():
                await_swap(slot)

            return product(held[jnp.where(is_panel(zz, q), panel, slot)], held[panel])

        asend[j] = piece(second_of(j), 2 * j + 1).astype(BF16)
        a_copy(j).start()
        part[0, j] = piece(a, 2 * j)

    def gram_c(j):
        zz = part_at(j)

        @pl.when(j == 0)
        def _():
            await_gather(4)

        @pl.when(other_than_panel(zz, a))
        def _():
            await_gather(j)

        part[1, j] = product(gathered[jnp.where(is_panel(zz, a), 4, j)], gathered[4])
        for bb in range(4):
            bsend[1, j, bb] = part[1, j, pl.ds(bb * 96, 96), :].astype(BF16)
        for o in (2, 1, 3):
            b_copy(1, j, o).start()

    def b_copy(f, j, o):
        bb = (b + o) % 4
        return pltpu.make_async_remote_copy(
            src_ref=bsend.at[f, j, bb],
            dst_ref=brecv.at[f, j, o - 1],
            send_sem=b_sent.at[f],
            recv_sem=b_in.at[f, j],
            device_id=peer_b(bb),
            device_id_type=MESH,
        )

    def sum_a(j):
        a_copy(j).wait_recv()
        for bb in range(4):
            rows = pl.ds(bb * 96, 96)
            total = part[0, j, rows, :] + arecv[j, rows, :].astype(F32)
            part[0, j, rows, :] = total
            bsend[0, j, bb] = total.astype(BF16)
        for o in (2, 1, 3):
            b_copy(0, j, o).start()

    def c_copy(f, j):
        zz = part_at(j)
        return pltpu.make_async_remote_copy(
            src_ref=csend.at[f, j],
            dst_ref=crecv.at[f, jnp.where(zh < zz, zh, zh - 1)],
            send_sem=c_sent.at[f],
            recv_sem=c_got.at[f],
            device_id=owner(zz),
            device_id_type=MESH,
        )

    def meet_above():
        @pl.when(zh < 3)
        def _():
            pl.semaphore_wait(above, 3 - zh)

    def sum_b(f, j):
        pltpu.make_async_copy(brecv.at[f, j], brecv.at[f, j], b_in.at[f, j]).wait()
        total = part[f, j, pl.ds(pl.multiple_of(b * 96, 96), 96), :]
        for o in (1, 3, 2):
            total = total + brecv[f, j, o - 1].astype(F32)

        @pl.when(j == 3)
        def _():
            fin[f] = total

        @pl.when(j < 3)
        def _():
            csend[f, j] = total.astype(BF16)
            c_copy(f, j).start()

    def finish(f, out):
        pltpu.make_async_copy(crecv.at[f], crecv.at[f], c_got.at[f]).wait()
        total = fin[f]
        for j in range(3):
            total = total + crecv[f, j].astype(F32)
        out[...] = total

    words = [
        jnp.where(s == 0, w0, jnp.where(s == 1, w1, jnp.where(s == 2, w2, w3)))
        for w0, w1, w2, w3 in zip(*map(packed, (SECTION0, SECTION1, SECTION2, SECTION3)))
    ]

    def step(t, done):
        word = words[-1]
        for i in range(len(words) - 1):
            word = jnp.where(t // 3 == i, words[i], word)
        op = jnp.where(t % 3 == 0, word, jnp.where(t % 3 == 1, word // 256, word // 65536)) % 256
        kind, what = op // 32, op % 32
        upto = jnp.where(kind == RELAY, what, done)
        lax.fori_loop(done, upto, relay, 0)

        @pl.when(kind == HAND_C)
        def _():
            hand_c(what)

        @pl.when(kind == SWAP_X)
        def _():
            swap_x(what)

        @pl.when(kind == GRAM_X)
        def _():
            gram_x(what)

        @pl.when(kind == GRAM_C)
        def _():
            gram_c(what)

        @pl.when(kind == SUM_A)
        def _():
            sum_a(what)

        @pl.when(kind == MEET)
        def _():
            meet_above()

        @pl.when(kind == SUM_B)
        def _():
            sum_b(what // 4, what % 4)

        return upto

    lax.fori_loop(0, 3 * len(words), step, jnp.int32(0))
    finish(0, in_out)
    finish(1, grad_out)

    def await_sent(ref, sem):
        pltpu.make_async_copy(ref, ref, sem).wait()

    swaps = jnp.logical_and(core == 0, jnp.logical_and(a != 0, second_of(panel_part) != 0))
    hands = jnp.logical_and(core == 0, a != 0)
    for less, count, sem in ((swaps, 10, swap_sent), (hands, 15, gather_sent)):

        @pl.when(less)
        def _():
            await_sent(xbuf.at[pl.ds(0, count - 1)], sem)

        @pl.when(jnp.logical_not(less))
        def _():
            await_sent(xbuf.at[pl.ds(0, count)], sem)

    await_sent(asend, a_sent)
    for f in range(2):
        await_sent(bsend.at[f, pl.ds(0, 3)], b_sent.at[f])
        await_sent(csend.at[f], c_sent.at[f])

    @pl.when(s > 0)
    def _():
        await_sent(obuf, relay_sent)


def body(activations, top_cotangent, branch_gains):
    width = activations.shape[-1]
    total_rows = ROWS * lax.axis_size("dp")
    dma = pltpu.SemaphoreType.DMA
    sums = pl.pallas_call(
        kernel,
        out_shape=[jax.ShapeDtypeStruct((96, PANEL), F32)] * 2,
        in_specs=[
            pl.BlockSpec(memory_space=pl.ANY),
            pl.BlockSpec(memory_space=pl.ANY),
            pl.BlockSpec(memory_space=pl.ANY),
        ],
        out_specs=[pl.BlockSpec(memory_space=pltpu.VMEM)] * 2,
        scratch_shapes=[
            pltpu.VMEM((BLOCKS, 1, PANEL), F32),
            pltpu.VMEM((2, BLOCKS, ROWS, PANEL), BF16),
            pltpu.VMEM((2, BLOCKS, ROWS, PANEL), BF16),
            pltpu.VMEM((BLOCKS, ROWS, PANEL), BF16),
            pltpu.VMEM((10, 2 * ROWS, PANEL), BF16),
            pltpu.VMEM((5, 4 * ROWS, PANEL), BF16),
            pltpu.VMEM((2, 4, PANEL, PANEL), F32),
            pltpu.VMEM((4, PANEL, PANEL), BF16),
            pltpu.VMEM((4, PANEL, PANEL), BF16),
            pltpu.VMEM((2, 4, 4, 96, PANEL), BF16),
            pltpu.VMEM((2, 4, 3, 96, PANEL), BF16),
            pltpu.VMEM((2, 3, 96, PANEL), BF16),
            pltpu.VMEM((2, 3, 96, PANEL), BF16),
            pltpu.VMEM((2, 96, PANEL), F32),
            dma,
            dma,
            dma((BLOCKS,)),
            dma,
            dma,
            dma((10,)),
            dma,
            dma((5,)),
            dma,
            dma((4,)),
            dma((2,)),
            dma((2, 4)),
            dma((2,)),
            dma((2,)),
            pltpu.SemaphoreType.REGULAR,
        ],
        compiler_params=pltpu.CompilerParams(
            collective_id=0, has_side_effects=True, vmem_limit_bytes=53 * 2**20
        ),
        cost_estimate=pl.CostEstimate(
            flops=4 * ROWS * width * PANEL,
            bytes_accessed=4 * ROWS * width,
            transcendentals=2 * ROWS * width,
        ),
    )(
        activations.reshape(ROWS, width),
        top_cotangent.reshape(ROWS, width),
        branch_gains.reshape(BLOCKS, 1, PANEL),
    )
    return tuple((total / F32(total_rows))[None] for total in sums)


def solution(mesh):
    in_specs = (P("section", None, "dp", None), P(None, "dp", None), P("section", None))
    out_specs = (P("section", "dp", None), P("section", "dp", None))
    return jax.shard_map(
        body,
        mesh=mesh,
        in_specs=in_specs,
        out_specs=out_specs,
        check_vma=False,
    )
```

```python
import jax
import jax.numpy as jnp
from jax import lax
from jax.experimental import pallas as pl
from jax.experimental.pallas import tpu as pltpu
from jax.sharding import PartitionSpec as P

PANEL = 384
ROWS = 224
BLOCKS = 16
SLAB = 32
SORTED = 112
KINDS = RELAY, HAND_C, GRAM_X, GRAM_C, SUM_A, SUM_B, MEET, SWAP_X = range(8)
R, S, G, D, A, B, M, X = (32 * kind for kind in KINDS)
SECTION3 = (R + 2, X + 0, R + 4, X + 1, R + 6, X + 2, R + 8, X + 3, R + 16, G + 0, G + 1, G + 2, G + 3, S + 0, S + 1, A + 0, A + 1, A + 2, A + 3, S + 2, D + 0, S + 3, D + 1, M + 0, B + 0, B + 1, B + 2, B + 3, B + 4, D + 2, B + 5, D + 3, B + 6, B + 7)
SECTION2 = (X + 0, X + 1, X + 2, X + 3, R + 16, G + 0, G + 1, G + 2, G + 3, S + 0, S + 1, A + 0, A + 1, A + 2, A + 3, S + 2, D + 0, S + 3, D + 1, M + 0, B + 0, B + 1, B + 2, B + 3, B + 4, D + 2, B + 5, D + 3, B + 6, B + 7)
SECTION1 = (X + 0, X + 1, X + 2, X + 3, R + 4, G + 0, G + 1, R + 5, S + 0, G + 2, G + 3, R + 9, S + 1, A + 0, R + 10, A + 1, D + 0, A + 2, A + 3, R + 13, S + 2, D + 1, M + 0, B + 0, B + 1, B + 4, R + 16, S + 3, D + 2, B + 2, B + 3, B + 5, D + 3, B + 6, B + 7)
SECTION0 = (X + 0, X + 1, X + 2, X + 3, R + 4, G + 0, G + 1, R + 5, S + 0, G + 2, G + 3, R + 9, S + 1, A + 0, R + 10, A + 1, D + 0, A + 2, A + 3, R + 13, S + 2, D + 1, M + 0, B + 0, B + 1, B + 4, R + 16, S + 3, D + 2, B + 2, B + 3, B + 5, D + 3, B + 6, B + 7)
WORDS = 15
MESH = pl.DeviceIdType.MESH
F32 = jnp.float32
BF16 = jnp.bfloat16


def packed(ops):
    codes = ops + (R + BLOCKS,) * (3 * WORDS - len(ops))
    return [codes[i] + 256 * codes[i + 1] + 65536 * codes[i + 2] for i in range(0, len(codes), 3)]


def gelu_slope(values):
    return (
        0.5 * (1.0 + lax.erf(values * 0.7071067811865476))
        + values * jnp.exp(-0.5 * values * values) * 0.3989422804014327
    )


def kernel(
    x_hbm,
    top_hbm,
    gains_hbm,
    in_out,
    grad_out,
    gains,
    whole,
    sorted_by_x,
    obuf,
    held,
    gathered,
    part,
    asend,
    arecv,
    bsend,
    brecv,
    csend,
    crecv,
    fin,
    gain_load,
    x_load,
    c_in,
    relay_sent,
    swap_sent,
    swap_in,
    gather_sent,
    gather_in,
    a_sent,
    a_in,
    b_sent,
    b_in,
    c_sent,
    c_got,
    above,
):
    s = lax.axis_index("section")
    d = lax.axis_index("dp")
    core = s % 2
    zh, y, x = d // 16, (d // 4) % 4, d % 4
    a = jnp.where(core == 0, y, x)
    b = jnp.where(core == 0, x, y)
    xbuf, cbuf = whole.at[0], whole.at[1]

    def at(zz, aa, bb):
        return zz * 16 + jnp.where(core == 0, aa * 4 + bb, bb * 4 + aa)

    def peer_a(aa):
        return (s, at(zh, aa, b))

    def peer_b(bb):
        return (s, at(zh, a, bb))

    def owner(zz):
        return (s, at(zz, a, b))

    flip, mirror = a + 1 - 2 * (a % 2), 3 - a
    opposite = (a + 2) % 4

    def first_of(j):
        return jnp.where(j % 2 == 0, flip, mirror)

    def second_of(j):
        return jnp.where(j % 2 == 0, mirror, flip)

    barrier = pltpu.get_barrier_semaphore()

    def greet(device):
        pl.semaphore_signal(barrier, inc=1, device_id=device, device_id_type=MESH)

    greet(peer_a(flip))
    greet(peer_a(mirror))
    greet(peer_a(opposite))
    for o in (1, 2, 3):
        greet(peer_b((b + o) % 4))

        @pl.when(zh + o < 4)
        def _():
            greet(owner(zh + o))

    @pl.when(s > 0)
    def _():
        greet((s - 1, d))

    @pl.when(s < 3)
    def _():
        greet((s + 1, d))

    def part_at(j):
        return jnp.where(j == 3, zh, jnp.where(j < zh, j, j + 1))

    panel_part = jnp.where(zh == 0, 3, 0)
    first = 4 * panel_part + (8 - x - y) % 4

    def block_at(p):
        i = jnp.where(p == 0, first, jnp.where(p <= first, p - 1, p))
        return part_at(i // 4) * 4 + (i + x + y) % 4

    def columns(blk):
        return pl.ds(pl.multiple_of(blk * PANEL, PANEL), PANEL)

    def load(p, _):
        blk = block_at(p)

        @pl.when(s > 0)
        def _():
            pltpu.make_async_copy(x_hbm.at[:, columns(blk)], xbuf.at[blk], x_load).start()

        @pl.when(s == 3)
        def _():
            pltpu.make_async_copy(top_hbm.at[:, columns(blk)], cbuf.at[blk], c_in.at[blk]).start()

        return 0

    lax.fori_loop(0, BLOCKS, load, 0)
    pltpu.make_async_copy(gains_hbm, gains, gain_load).start()

    others = 6 + zh + jnp.where(s > 0, 1, 0) + jnp.where(s < 3, 1, 0)
    pl.semaphore_wait(barrier, others)

    for o in (1, 2, 3):

        @pl.when(zh >= o)
        def _():
            pl.semaphore_signal(above, inc=1, device_id=owner(zh - o), device_id_type=MESH)


    def swap(src, slot, aa):
        return pltpu.make_async_remote_copy(
            src_ref=src,
            dst_ref=held.at[slot, pl.ds(ROWS, ROWS), :],
            send_sem=swap_sent,
            recv_sem=swap_in.at[slot],
            device_id=peer_a(aa),
            device_id_type=MESH,
        )

    def keep(src, slot):
        return pltpu.make_async_copy(src, held.at[slot, pl.ds(0, ROWS), :], swap_in.at[slot])

    def is_panel(zz, q):
        return jnp.logical_and(core == 0, jnp.logical_and(zz == 0, q == 0))

    def other_than_panel(zz, q):
        return jnp.logical_not(is_panel(zz, q))

    def swap_part(j, piece):
        zz = part_at(j)
        to = first_of(j)
        for q, slot in ((opposite, 2 * j + 1), (to, 2 * j)):

            @pl.when(other_than_panel(zz, q))
            def _():
                swap(piece(zz * 4 + q), slot, to).start()

        for q, slot in ((second_of(j), 2 * j + 1), (a, 2 * j)):

            @pl.when(other_than_panel(zz, q))
            def _():
                keep(piece(zz * 4 + q), slot).start()

    def rows_of(aa):
        return pl.ds(pl.multiple_of(aa * ROWS, ROWS), ROWS)

    def hand(src, slot, aa):
        return pltpu.make_async_remote_copy(
            src_ref=src,
            dst_ref=gathered.at[slot, rows_of(a), :],
            send_sem=gather_sent,
            recv_sem=gather_in.at[slot],
            device_id=peer_a(aa),
            device_id_type=MESH,
        )

    def hold(src, slot):
        return pltpu.make_async_copy(src, gathered.at[slot, rows_of(a), :], gather_in.at[slot])

    def hand_part(j, piece):
        zz = part_at(j)
        for o in (2, 1, 3):
            aa = (a + o) % 4

            @pl.when(other_than_panel(zz, aa))
            def _():
                hand(piece(zz * 4 + aa), j, aa).start()

        @pl.when(other_than_panel(zz, a))
        def _():
            hold(piece(zz * 4 + a), j).start()

    def sort_part(f, j):
        zz = part_at(j)

        def sort(i, _):
            rows = pl.ds(pl.multiple_of(i * SORTED, SORTED), SORTED)
            blocks = [whole[f, zz * 4 + yy, rows, :].astype(F32) for yy in range(4)]
            for xx in range(4):
                sorted_by_x[f, zz * 4 + xx, rows, :] = jnp.concatenate(
                    [block[:, xx * 96 : xx * 96 + 96] for block in blocks], axis=1
                ).astype(BF16)
            return 0

        lax.fori_loop(0, ROWS // SORTED, sort, 0)

    x_panel = x_hbm.at[:, pl.ds(0, PANEL)]
    swap(x_panel, 8, flip).start()
    swap(x_panel, 9, mirror).start()
    keep(x_panel, 8).start()
    keep(x_panel, 9).start()

    def swap_x(j):
        @pl.when(core == 0)
        def _():
            swap_part(j, lambda blk: x_hbm.at[:, columns(blk)])

        @pl.when(core == 1)
        def _():
            sort_part(0, j)
            swap_part(j, lambda blk: sorted_by_x.at[0, blk])

    @pl.when(s > 0)
    def _():
        pltpu.make_async_copy(xbuf, xbuf, x_load).wait()

    pltpu.make_async_copy(gains_hbm, gains, gain_load).wait()

    def relay_copy(blk):
        return pltpu.make_async_remote_copy(
            src_ref=obuf.at[blk],
            dst_ref=cbuf.at[blk],
            send_sem=relay_sent,
            recv_sem=c_in.at[blk],
            device_id=(s - 1, d),
            device_id_type=MESH,
        )

    def relay(p, _):
        blk = block_at(p)
        pltpu.make_async_copy(cbuf.at[blk], cbuf.at[blk], c_in.at[blk]).wait()

        @pl.when(p == 0)
        def _():
            for o in (2, 1, 3):
                hand(cbuf.at[blk], 4, (a + o) % 4).start()
            hold(cbuf.at[blk], 4).start()

        @pl.when(s > 0)
        def _():
            gain = gains[blk]

            def slab(i, _):
                rows = pl.ds(pl.multiple_of(i * SLAB, SLAB), SLAB)
                scaling = 1.0 + gain * gelu_slope(xbuf[blk, rows, :].astype(F32))
                obuf[blk, rows, :] = (cbuf[blk, rows, :].astype(F32) * scaling).astype(BF16)
                return 0

            lax.fori_loop(0, ROWS // SLAB, slab, 0)
            relay_copy(blk).start()

        return 0

    def hand_c(j):
        @pl.when(core == 0)
        def _():
            hand_part(j, lambda blk: cbuf.at[blk])

        @pl.when(core == 1)
        def _():
            sort_part(1, j)
            hand_part(j, lambda blk: sorted_by_x.at[1, blk])

    def await_swap(slot):
        pltpu.make_async_copy(held.at[slot], held.at[slot], swap_in.at[slot]).wait()

    def await_gather(slot):
        pltpu.make_async_copy(gathered.at[slot], gathered.at[slot], gather_in.at[slot]).wait()

    def product(left, right):
        return lax.dot_general(left, right, (((0,), (0,)), ((), ())), preferred_element_type=F32)

    def a_copy(j):
        return pltpu.make_async_remote_copy(
            src_ref=asend.at[j],
            dst_ref=arecv.at[j],
            send_sem=a_sent,
            recv_sem=a_in.at[j],
            device_id=peer_a(second_of(j)),
            device_id_type=MESH,
        )

    def gram_x(j):
        zz = part_at(j)
        panel = 8 + j % 2

        @pl.when(j < 2)
        def _():
            await_swap(panel)

        def piece(q, slot):
            @pl.when(other_than_panel(zz, q))
            def _():
                await_swap(slot)

            return product(held[jnp.where(is_panel(zz, q), panel, slot)], held[panel])

        asend[j] = piece(second_of(j), 2 * j + 1).astype(BF16)
        a_copy(j).start()
        part[0, j] = piece(a, 2 * j)

    def gram_c(j):
        zz = part_at(j)

        @pl.when(j == 0)
        def _():
            await_gather(4)

        @pl.when(other_than_panel(zz, a))
        def _():
            await_gather(j)

        part[1, j] = product(gathered[jnp.where(is_panel(zz, a), 4, j)], gathered[4])
        for bb in range(4):
            bsend[1, j, bb] = part[1, j, pl.ds(bb * 96, 96), :].astype(BF16)
        for o in (2, 1, 3):
            b_copy(1, j, o).start()

    def b_copy(f, j, o):
        bb = (b + o) % 4
        return pltpu.make_async_remote_copy(
            src_ref=bsend.at[f, j, bb],
            dst_ref=brecv.at[f, j, o - 1],
            send_sem=b_sent.at[f],
            recv_sem=b_in.at[f, j],
            device_id=peer_b(bb),
            device_id_type=MESH,
        )

    def sum_a(j):
        a_copy(j).wait_recv()
        for bb in range(4):
            rows = pl.ds(bb * 96, 96)
            total = part[0, j, rows, :] + arecv[j, rows, :].astype(F32)
            part[0, j, rows, :] = total
            bsend[0, j, bb] = total.astype(BF16)
        for o in (2, 1, 3):
            b_copy(0, j, o).start()

    def c_copy(f, j):
        zz = part_at(j)
        return pltpu.make_async_remote_copy(
            src_ref=csend.at[f, j],
            dst_ref=crecv.at[f, jnp.where(zh < zz, zh, zh - 1)],
            send_sem=c_sent.at[f],
            recv_sem=c_got.at[f],
            device_id=owner(zz),
            device_id_type=MESH,
        )

    def meet_above():
        @pl.when(zh < 3)
        def _():
            pl.semaphore_wait(above, 3 - zh)

    def sum_b(f, j):
        pltpu.make_async_copy(brecv.at[f, j], brecv.at[f, j], b_in.at[f, j]).wait()
        total = part[f, j, pl.ds(pl.multiple_of(b * 96, 96), 96), :]
        for o in (1, 3, 2):
            total = total + brecv[f, j, o - 1].astype(F32)

        @pl.when(j == 3)
        def _():
            fin[f] = total

        @pl.when(j < 3)
        def _():
            csend[f, j] = total.astype(BF16)
            c_copy(f, j).start()

    def finish(f, out):
        pltpu.make_async_copy(crecv.at[f], crecv.at[f], c_got.at[f]).wait()
        total = fin[f]
        for j in range(3):
            total = total + crecv[f, j].astype(F32)
        out[...] = total

    words = [
        jnp.where(s == 0, w0, jnp.where(s == 1, w1, jnp.where(s == 2, w2, w3)))
        for w0, w1, w2, w3 in zip(*map(packed, (SECTION0, SECTION1, SECTION2, SECTION3)))
    ]

    def step(t, done):
        word = words[-1]
        for i in range(len(words) - 1):
            word = jnp.where(t // 3 == i, words[i], word)
        op = jnp.where(t % 3 == 0, word, jnp.where(t % 3 == 1, word // 256, word // 65536)) % 256
        kind, what = op // 32, op % 32
        upto = jnp.where(kind == RELAY, what, done)
        lax.fori_loop(done, upto, relay, 0)

        @pl.when(kind == HAND_C)
        def _():
            hand_c(what)

        @pl.when(kind == SWAP_X)
        def _():
            swap_x(what)

        @pl.when(kind == GRAM_X)
        def _():
            gram_x(what)

        @pl.when(kind == GRAM_C)
        def _():
            gram_c(what)

        @pl.when(kind == SUM_A)
        def _():
            sum_a(what)

        @pl.when(kind == MEET)
        def _():
            meet_above()

        @pl.when(kind == SUM_B)
        def _():
            sum_b(what // 4, what % 4)

        return upto

    lax.fori_loop(0, 3 * len(words), step, jnp.int32(0))
    finish(0, in_out)
    finish(1, grad_out)

    def await_sent(ref, sem):
        pltpu.make_async_copy(ref, ref, sem).wait()

    swaps = jnp.logical_and(core == 0, jnp.logical_and(a != 0, second_of(panel_part) != 0))
    hands = jnp.logical_and(core == 0, a != 0)
    for less, count, sem in ((swaps, 10, swap_sent), (hands, 15, gather_sent)):

        @pl.when(less)
        def _():
            await_sent(xbuf.at[pl.ds(0, count - 1)], sem)

        @pl.when(jnp.logical_not(less))
        def _():
            await_sent(xbuf.at[pl.ds(0, count)], sem)

    await_sent(asend, a_sent)
    for f in range(2):
        await_sent(bsend.at[f, pl.ds(0, 3)], b_sent.at[f])
        await_sent(csend.at[f], c_sent.at[f])

    @pl.when(s > 0)
    def _():
        await_sent(obuf, relay_sent)


def body(activations, top_cotangent, branch_gains):
    width = activations.shape[-1]
    total_rows = ROWS * lax.axis_size("dp")
    dma = pltpu.SemaphoreType.DMA
    sums = pl.pallas_call(
        kernel,
        out_shape=[jax.ShapeDtypeStruct((96, PANEL), F32)] * 2,
        in_specs=[
            pl.BlockSpec(memory_space=pl.ANY),
            pl.BlockSpec(memory_space=pl.ANY),
            pl.BlockSpec(memory_space=pl.ANY),
        ],
        out_specs=[pl.BlockSpec(memory_space=pltpu.VMEM)] * 2,
        scratch_shapes=[
            pltpu.VMEM((BLOCKS, 1, PANEL), F32),
            pltpu.VMEM((2, BLOCKS, ROWS, PANEL), BF16),
            pltpu.VMEM((2, BLOCKS, ROWS, PANEL), BF16),
            pltpu.VMEM((BLOCKS, ROWS, PANEL), BF16),
            pltpu.VMEM((10, 2 * ROWS, PANEL), BF16),
            pltpu.VMEM((5, 4 * ROWS, PANEL), BF16),
            pltpu.VMEM((2, 4, PANEL, PANEL), F32),
            pltpu.VMEM((4, PANEL, PANEL), BF16),
            pltpu.VMEM((4, PANEL, PANEL), BF16),
            pltpu.VMEM((2, 4, 4, 96, PANEL), BF16),
            pltpu.VMEM((2, 4, 3, 96, PANEL), BF16),
            pltpu.VMEM((2, 3, 96, PANEL), BF16),
            pltpu.VMEM((2, 3, 96, PANEL), BF16),
            pltpu.VMEM((2, 96, PANEL), F32),
            dma,
            dma,
            dma((BLOCKS,)),
            dma,
            dma,
            dma((10,)),
            dma,
            dma((5,)),
            dma,
            dma((4,)),
            dma((2,)),
            dma((2, 4)),
            dma((2,)),
            dma((2,)),
            pltpu.SemaphoreType.REGULAR,
        ],
        compiler_params=pltpu.CompilerParams(
            collective_id=0, has_side_effects=True, vmem_limit_bytes=53 * 2**20
        ),
        cost_estimate=pl.CostEstimate(
            flops=4 * ROWS * width * PANEL,
            bytes_accessed=4 * ROWS * width,
            transcendentals=2 * ROWS * width,
        ),
    )(
        activations.reshape(ROWS, width),
        top_cotangent.reshape(ROWS, width),
        branch_gains.reshape(BLOCKS, 1, PANEL),
    )
    return tuple((total / F32(total_rows))[None] for total in sums)


def solution(mesh):
    in_specs = (P("section", None, "dp", None), P(None, "dp", None), P("section", None))
    out_specs = (P("section", "dp", None), P("section", "dp", None))
    return jax.shard_map(
        body,
        mesh=mesh,
        in_specs=in_specs,
        out_specs=out_specs,
        check_vma=False,
    )
```
